128 devices in a mesh: user: 16 (over z, y_lo, core), item: 8 (over x, y_hi).
Axes of the slice: x: 4, y: 4 (y_hi: 2, y_lo: 2; y = y_hi * 2 + y_lo), z: 4, core: 2. Of those that a mesh axis runs over, the one named last changes fastest.
Arguments:
- user_table: float32 [16384, 256], P(('user', 'item')), may hold values from -1.5 to 1.5
- user_state: float32 [16384], P(('user', 'item')), may hold values from 0.001 to 0.1
- item_table: float32 [32768, 256], P(('item', 'user')), may hold values from -1.5 to 1.5
- item_state: float32 [32768], P(('item', 'user')), may hold values from 0.001 to 0.1
- edge_users: int32 [16, 8, 2048], P('user', 'item'), may hold values from 0 to 1023
- edge_items: int32 [16, 8, 2048], P('user', 'item'), may hold values from 0 to 4095
- negatives: int32 [8, 1024], P('item'), may hold values from 0 to 4095
Outputs:
- new_user_table: float32 [16384, 256], P(('user', 'item'))
- new_user_state: float32 [16384], P(('user', 'item'))
- new_item_table: float32 [32768, 256], P(('item', 'user'))
- new_item_state: float32 [32768], P(('item', 'user'))
The draws below stay inside these ranges and needn't reach their ends.
All inputs are finite; a program needn't handle non-finite values.
Results may differ from the reference program's by a relative error of at most 0.0017.
Values may be sent and summed in bfloat16 or wider, within the bound.
A program may use at most 64 MiB of HBM per device.

```python
import math
import jax
import jax.numpy as jnp
from jax import lax

D = 256
EDGES = 2048
NEG = 1024
UR_DEV = 128
IR_DEV = 256
PU = 1024
PI = 4096
NU = 16384
NI = 32768
N_USER = 16
N_ITEM = 8


def plant(array, own_key, least, top_value):
    place = [jax.random.randint(jax.random.fold_in(own_key, axis), (), 0, length) for axis, length in enumerate(array.shape)]
    main_axis = array.shape.index(max(array.shape))
    beside = place[:main_axis] + [(place[main_axis] + 1) % array.shape[main_axis]] + place[main_axis + 1:]
    return array.at[tuple(place)].set(least).at[tuple(beside)].set(top_value)


def levels(stream_key, extent, shards, smallest, top_value):
    def one(position, parts):
        heights = jax.random.uniform(jax.random.fold_in(jax.random.fold_in(stream_key, 6), position), (parts,), jnp.float32, smallest / len(shards), top_value / len(shards))
        return jnp.repeat(jnp.exp(heights), extent[position] // parts).reshape((-1,) + (1,) * (len(extent) - position - 1))

    level = one(*shards[0])
    for cut in shards[1:]:
        level = level * one(*cut)
    return level


def normal_values(stream_key, shape, scale, bound, cuts=(), kind=jnp.bfloat16):
    array = jax.random.normal(stream_key, shape, jnp.float32) * scale
    if len(cuts) > 0:
        array = levels(stream_key, shape, cuts, -0.22, 0.18) * array
    return jnp.clip(array, min=-bound, max=bound).astype(kind)


def setup_inputs(seed: int = 0) -> dict:
    key_of = jax.random.split(jax.random.key(seed), 8)
    user_table = normal_values(key_of[0], (NU, D), 0.25, 1.5, ((0, 128),), jnp.float32)
    user_state = jnp.clip(jnp.exp(math.log(0.1) - 4.6051702 * jax.random.uniform(key_of[1], (NU,), jnp.float32) ** levels(key_of[1], (NU,), ((0, 128),), -0.2, 0.2)), 0.001, 0.1)
    item_table = normal_values(key_of[2], (NI, D), 0.25, 1.5, ((0, 128),), jnp.float32)
    item_state = jnp.clip(jnp.exp(math.log(0.1) - 4.6051702 * jax.random.uniform(key_of[3], (NI,), jnp.float32) ** levels(key_of[3], (NI,), ((0, 128),), -0.2, 0.2)), 0.001, 0.1)
    edge_users = plant(jax.random.randint(key_of[4], (N_USER, N_ITEM, EDGES), 0, PU), jax.random.fold_in(key_of[4], 1), 0, PU - 1).astype(jnp.int32)
    edge_items = plant(jax.random.randint(key_of[5], (N_USER, N_ITEM, EDGES), 0, PI), jax.random.fold_in(key_of[5], 1), 0, PI - 1).astype(jnp.int32)
    negatives = plant(jax.random.randint(key_of[6], (N_ITEM, NEG), 0, PI), jax.random.fold_in(key_of[6], 1), 0, PI - 1).astype(jnp.int32)
    return dict(user_table=user_table, user_state=user_state, item_table=item_table, item_state=item_state, edge_users=edge_users, edge_items=edge_items, negatives=negatives)


learn_rate = 0.1

def adagrad(table, state, gradient):
    new_state = state + lax.optimization_barrier(jnp.mean(gradient * gradient, axis=1))
    return (table - learn_rate * gradient / jnp.sqrt(new_state)[:, None], new_state)

def reference(user_table, user_state, item_table, item_state, edge_users, edge_items, negatives):
    part_users = UR_DEV * N_ITEM
    part_items = IR_DEV * N_USER
    user_low = user_table.astype(jnp.bfloat16)
    item_low = item_table.astype(jnp.bfloat16)

    def edge_block(block_number, totals):
        user_sums, item_sums = totals
        user_part = block_number // N_ITEM
        item_part = block_number % N_ITEM
        user_rows = edge_users[user_part, item_part].astype(jnp.int32) + (user_part * part_users).astype(jnp.int32)
        item_rows = edge_items[user_part, item_part].astype(jnp.int32) + (item_part * part_items).astype(jnp.int32)
        negative_rows = negatives[item_part].astype(jnp.int32) + (item_part * part_items).astype(jnp.int32)
        picked_users = user_low[user_rows]
        picked_items = item_low[item_rows]
        picked_negatives = item_low[negative_rows]
        positive = lax.optimization_barrier(jnp.sum(picked_users.astype(jnp.float32) * picked_items.astype(jnp.float32), axis=1))
        negative_scores = jnp.dot(picked_users, picked_negatives.T, preferred_element_type=jnp.float32)
        weights = (jax.nn.sigmoid(negative_scores) / NEG).astype(jnp.bfloat16)
        pull = jax.nn.sigmoid(-positive)[:, None]
        user_grad = (-pull * picked_items.astype(jnp.float32) + jnp.dot(weights, picked_negatives, preferred_element_type=jnp.float32)).astype(jnp.bfloat16)
        item_grad = (-pull * picked_users.astype(jnp.float32)).astype(jnp.bfloat16)
        negative_grad = jnp.dot(weights.T, picked_users, preferred_element_type=jnp.float32).astype(jnp.bfloat16)
        user_sums = user_sums.at[user_rows].add(user_grad.astype(jnp.float32))
        item_sums = item_sums.at[item_rows].add(item_grad.astype(jnp.float32))
        item_sums = item_sums.at[negative_rows].add(negative_grad.astype(jnp.float32))
        return (user_sums, item_sums)
    start_sums = (jnp.zeros(user_table.shape, jnp.float32), jnp.zeros(item_table.shape, jnp.float32))
    user_total, item_total = lax.fori_loop(0, N_USER * N_ITEM, edge_block, start_sums)
    new_user_table, new_user_state = adagrad(user_table, user_state, user_total)
    new_item_table, new_item_state = adagrad(item_table, item_state, item_total)
    return (new_user_table, new_user_state, new_item_table, new_item_state)
```

```python
import jax
import jax.numpy as jnp
from jax import lax
from jax.experimental import pallas as pl
from jax.experimental.pallas import tpu as pltpu
from jax.sharding import PartitionSpec as P

learn_rate = 0.1
MESH = pl.DeviceIdType.MESH
BF = jnp.bfloat16
F32 = jnp.float32

D = 256
EDGES = 2048
NEG = 1024
PICKS = EDGES + NEG
UR = 128
IR = 256
PLANE = 4 * IR
BLK = 256


def one_hot_cols(index, width):
    lane = lax.broadcasted_iota(jnp.int32, index.shape, 1)
    parts = [
        jnp.where(index == lane + 128 * c, F32(1), F32(0)).astype(BF) for c in range(width // 128)
    ]
    return jnp.concatenate(parts, axis=1)


def one_hot_rows(index, base, rows):
    row = lax.broadcasted_iota(jnp.int32, (rows, index.shape[1]), 0) + base
    return jnp.where(row == index, F32(1), F32(0)).astype(BF)


def to_column(row):
    return jnp.broadcast_to(row, (128, 128)).T


def adagrad(table, state_ref, total, out_ref, out_state_ref):
    rows = total.shape[0]
    mean = jnp.sum(total * total, axis=1, keepdims=True) * (1.0 / D)
    for b in range(rows // 128):
        part = slice(128 * b, 128 * (b + 1))
        new_state = to_column(state_ref[:, part]) + mean[part]
        out_state_ref[:, part] = new_state.T[0:1, :]
        scale = learn_rate / jnp.sqrt(new_state)
        out_ref[part, :] = table[part, :] - total[part] * jnp.concatenate([scale, scale], axis=1)


def kernel(
    user_table, user_state, item_table, item_state, edge_users, edge_items, negatives,
    new_user_table, new_user_state, new_item_table, new_item_state,
    items, users, user_col, item_col, item_row, picked, picked_users, picked_negs, neg_grad,
    user_grad, item_grad,
    user_keep, u2s, u2r, uzs, uzr, uys, uyr,
    plane_sum, keep, sib_s, sib_r, z2s, z2r, zs, zr, ys, yr,
    send_sem, recv_sem,
):
    u, t = lax.axis_index("user"), lax.axis_index("item")
    k, yl, z = lax.rem(u, 2), lax.rem(lax.div(u, 2), 2), lax.div(u, 4)
    yh, x = lax.rem(t, 2), lax.div(t, 2)

    def user_id(zz, yy, kk):
        return (zz * 2 + yy) * 2 + kk

    def item_id(xx, yy):
        return xx * 2 + yy

    zp, zm, z2 = lax.rem(z + 1, 4), lax.rem(z + 3, 4), lax.rem(z + 2, 4)
    xp, xm, x2 = lax.rem(x + 1, 4), lax.rem(x + 3, 4), lax.rem(x + 2, 4)
    sib = {"user": user_id(z, yl, 1 - k)}
    yn = {"user": user_id(z, 1 - yl, k)}
    zup = {"user": user_id(zp, yl, k)}
    zdn = {"user": user_id(zm, yl, k)}
    hn = {"item": item_id(x, 1 - yh)}
    xup = {"item": item_id(xp, yh)}
    xdn = {"item": item_id(xm, yh)}

    barrier = pltpu.get_barrier_semaphore()
    for peer in (sib, yn, zup, zdn, hn, xup, xdn):
        pl.semaphore_signal(barrier, inc=1, device_id=peer, device_id_type=MESH)

    copies = []

    def message(src, dst, peer):
        n = len(copies)
        copy = pltpu.make_async_remote_copy(
            src_ref=src, dst_ref=dst, send_sem=send_sem.at[n], recv_sem=recv_sem.at[n],
            device_id=peer, device_id_type=MESH,
        )
        copies.append(copy)
        return copy

    def send(src, dst, peer):
        copy = message(src, dst, peer)
        copy.start()
        return copy

    items[u] = item_table[...].astype(BF)
    users[t] = user_table[...].astype(BF)
    pl.semaphore_wait(barrier, 7)

    def slot(ref, s):
        return ref.at[s]

    own_i, own_u = slot(items, u), slot(users, t)
    m_zup = send(own_i, own_i, zup)
    m_zdn = send(own_i, own_i, zdn)
    m_yn = send(own_i, own_i, yn)
    m_sib = send(own_i, own_i, sib)
    m_xup = send(own_u, own_u, xup)
    m_xdn = send(own_u, own_u, xdn)
    m_hn = send(own_u, own_u, hn)

    for b in range(EDGES // 128):
        part = slice(128 * b, 128 * (b + 1))
        user_col[part, :] = to_column(edge_users[0, :, part])
        item_col[part, :] = to_column(edge_items[0, :, part])
    for b in range(NEG // 128):
        item_col[EDGES + 128 * b:EDGES + 128 * (b + 1), :] = to_column(
            negatives[:, 128 * b:128 * (b + 1)]
        )
    item_row[:, :EDGES] = edge_items[0, :, :]
    item_row[:, EDGES:] = negatives[...]

    def pick_plane(zz, first):
        @pl.loop(0, PICKS // BLK)
        def _(b):
            rows = pl.ds(pl.multiple_of(b * BLK, BLK), BLK)
            one_hot = one_hot_cols(item_col[rows, :] - zz * PLANE, PLANE)
            plane = items[pl.ds(zz * 4, 4)].reshape(PLANE, D)
            got = jnp.dot(one_hot, plane, preferred_element_type=F32)
            picked[rows, :] = got if first else picked[rows, :] + got

    m_zup.wait_recv()
    s_zm = slot(items, user_id(zm, yl, k))
    lo, hi = pl.ds(0, IR // 2), pl.ds(IR // 2, IR // 2)
    m_z2a = send(s_zm.at[lo], s_zm.at[lo], zup)
    f_zm = send(s_zm, s_zm, sib)
    m_zdn.wait_recv()
    s_zp = slot(items, user_id(zp, yl, k))
    m_z2b = send(s_zp.at[hi], s_zp.at[hi], zdn)
    f_zp = send(s_zp, s_zp, sib)
    m_yn.wait_recv()
    s_yn = slot(items, user_id(z, 1 - yl, k))
    m_yzup = send(s_yn, s_yn, zup)
    m_yzdn = send(s_yn, s_yn, zdn)
    f_yn = send(s_yn, s_yn, sib)

    ulo, uhi = pl.ds(0, UR // 2), pl.ds(UR // 2, UR // 2)
    m_hn.wait_recv()
    s_hn = slot(users, item_id(x, 1 - yh))
    m_hxup = send(s_hn, s_hn, xup)
    m_hxdn = send(s_hn, s_hn, xdn)
    m_xup.wait_recv()
    s_xm = slot(users, item_id(xm, yh))
    m_x2a = send(s_xm.at[ulo], s_xm.at[ulo], xup)
    m_xdn.wait_recv()
    s_xp = slot(users, item_id(xp, yh))
    m_x2b = send(s_xp.at[uhi], s_xp.at[uhi], xdn)

    m_sib.wait_recv()
    f_yn.wait_recv()
    pick_plane(z, True)

    m_z2a.wait_recv()
    m_z2b.wait_recv()
    s_z2 = slot(items, user_id(z2, yl, k))
    m_z2y = send(s_z2, s_z2, yn)
    f_z2 = send(s_z2, s_z2, sib)
    m_hxup.wait_recv()
    s_hxm = slot(users, item_id(xm, 1 - yh))
    m_hx2a = send(s_hxm.at[ulo], s_hxm.at[ulo], xup)
    m_hxdn.wait_recv()
    s_hxp = slot(users, item_id(xp, 1 - yh))
    m_hx2b = send(s_hxp.at[uhi], s_hxp.at[uhi], xdn)

    m_yzup.wait_recv()
    s_yzm = slot(items, user_id(zm, 1 - yl, k))
    f_yzm = send(s_yzm, s_yzm, sib)
    m_yzdn.wait_recv()
    s_yzp = slot(items, user_id(zp, 1 - yl, k))
    f_yzp = send(s_yzp, s_yzp, sib)
    f_zm.wait_recv()
    f_yzm.wait_recv()
    pick_plane(zm, False)
    m_z2y.wait_recv()
    s_z2y = slot(items, user_id(z2, 1 - yl, k))
    f_z2y = send(s_z2y, s_z2y, sib)
    f_zp.wait_recv()
    f_yzp.wait_recv()
    pick_plane(zp, False)

    m_x2a.wait_recv()
    m_x2b.wait_recv()
    m_hx2a.wait_recv()
    m_hx2b.wait_recv()

    @pl.loop(0, EDGES // BLK)
    def _(b):
        rows = pl.ds(pl.multiple_of(b * BLK, BLK), BLK)
        one_hot = one_hot_cols(user_col[rows, :], 8 * UR)
        got = jnp.dot(one_hot, users[...].reshape(8 * UR, D), preferred_element_type=F32)
        picked_users[rows, :] = got.astype(BF)

    f_z2.wait_recv()
    f_z2y.wait_recv()
    pick_plane(z2, False)

    picked_negs[...] = picked[EDGES:, :].astype(BF)
    neg_grad[...] = jnp.zeros_like(neg_grad)

    @pl.loop(0, EDGES // BLK)
    def _(b):
        rows = pl.ds(pl.multiple_of(b * BLK, BLK), BLK)
        mine = picked_users[rows, :]
        wide = mine.astype(F32)
        item = picked[rows, :]
        negs = picked_negs[...]
        positive = jnp.sum(wide * item, axis=1, keepdims=True)
        pull = jax.nn.sigmoid(-positive)
        scores = lax.dot_general(mine, negs, (((1,), (1,)), ((), ())), preferred_element_type=F32)
        weights = (jax.nn.sigmoid(scores) * (1.0 / NEG)).astype(BF)
        user_grad[rows, :] = (
            -pull * item + jnp.dot(weights, negs, preferred_element_type=F32)
        ).astype(BF)
        item_grad[rows, :] = (-pull * wide).astype(BF)
        neg_grad[...] += lax.dot_general(
            weights, mine, (((0,), (0,)), ((), ())), preferred_element_type=F32
        )

    item_grad[EDGES:, :] = neg_grad[...].astype(BF)

    def spread_users(xx):
        one_hot = one_hot_rows(edge_users[0, :, :], xx * (2 * UR), 2 * UR)
        return jnp.dot(one_hot, user_grad[...], preferred_element_type=F32)

    got = spread_users(x2).astype(BF)
    u2s[...] = got.reshape(2, UR, D)
    m_u2p = send(u2s.at[0], u2r.at[0], xup)
    m_u2m = send(u2s.at[1], u2r.at[1], xdn)
    for n, xx in enumerate((xp, xm, x)):
        user_keep[n] = spread_users(xx).reshape(2, UR, D)

    def spread_items(zz, n):
        for m in range(4):
            @pl.loop(0, PICKS // 512)
            def _(c, m=m):
                part = pl.ds(pl.multiple_of(c * 512, 512), 512)
                one_hot = one_hot_rows(item_row[:, part], zz * PLANE + m * IR, IR)
                got = jnp.dot(one_hot, item_grad[part, :], preferred_element_type=F32)
                plane_sum[m] = jnp.where(c == 0, got, plane_sum[m] + got)
        for yy in range(2):
            sib_s[n, yy] = plane_sum[2 * yy + 1 - k].astype(BF)
            keep[n, yy] = plane_sum[2 * yy + k]
        return send(sib_s.at[n], sib_r.at[n], sib)

    m_s0 = spread_items(z2, 0)

    m_u2p.wait_recv()
    m_u2m.wait_recv()
    uzs[0, 0] = (user_keep[0, 0] + u2r[0].astype(F32)).astype(BF)
    uzs[0, 1] = user_keep[0, 1].astype(BF)
    m_uzp = send(uzs.at[0], uzr.at[0], xup)
    uzs[1, 0] = user_keep[1, 0].astype(BF)
    uzs[1, 1] = (user_keep[1, 1] + u2r[1].astype(F32)).astype(BF)
    m_uzm = send(uzs.at[1], uzr.at[1], xdn)

    m_s0.wait_recv()
    z2s[...] = (keep[0] + sib_r[0].astype(F32)).astype(BF)
    m_z2p = send(z2s.at[0], z2r.at[0], zup)
    m_z2m = send(z2s.at[1], z2r.at[1], zdn)

    m_s1 = spread_items(zp, 1)
    m_s2 = spread_items(zm, 2)

    m_s1.wait_recv()
    m_z2p.wait_recv()
    zs[0, 0] = (keep[1, 0] + sib_r[1, 0].astype(F32) + z2r[0].astype(F32)).astype(BF)
    zs[0, 1] = (keep[1, 1] + sib_r[1, 1].astype(F32)).astype(BF)
    m_zp = send(zs.at[0], zr.at[0], zup)
    m_s2.wait_recv()
    m_z2m.wait_recv()
    zs[1, 0] = (keep[2, 0] + sib_r[2, 0].astype(F32)).astype(BF)
    zs[1, 1] = (keep[2, 1] + sib_r[2, 1].astype(F32) + z2r[1].astype(F32)).astype(BF)
    m_zm = send(zs.at[1], zr.at[1], zdn)

    m_s3 = spread_items(z, 3)

    m_uzp.wait_recv()
    m_uzm.wait_recv()
    user_keep[2] = user_keep[2] + uzr[0].astype(F32) + uzr[1].astype(F32)
    uys[...] = user_keep[2, 1 - yh].astype(BF)
    m_uy = send(uys, uyr, hn)

    m_s3.wait_recv()
    keep[3] = keep[3] + sib_r[3].astype(F32)
    m_zp.wait_recv()
    m_zm.wait_recv()
    ys[...] = (keep[3, 1 - yl] + zr[0, 1 - yl].astype(F32) + zr[1, 1 - yl].astype(F32)).astype(BF)
    m_y = send(ys, yr, yn)
    keep[3, yl] = keep[3, yl] + zr[0, yl].astype(F32) + zr[1, yl].astype(F32)

    m_uy.wait_recv()
    adagrad(
        user_table, user_state, user_keep[2, yh] + uyr[...].astype(F32),
        new_user_table, new_user_state,
    )
    m_y.wait_recv()
    adagrad(
        item_table, item_state, keep[3, yl] + yr[...].astype(F32), new_item_table, new_item_state
    )
    for copy in copies:
        copy.wait_send()


MESSAGES = 40


def per_device(user_table, user_state, item_table, item_state, edge_users, edge_items, negatives):
    vmem = pl.BlockSpec(memory_space=pltpu.VMEM)
    scratch = [
        ((16, IR, D), BF),
        ((8, UR, D), BF),
        ((EDGES, 128), jnp.int32),
        ((PICKS, 128), jnp.int32),
        ((1, PICKS), jnp.int32),
        ((PICKS, D), F32),
        ((EDGES, D), BF),
        ((NEG, D), BF),
        ((NEG, D), F32),
        ((EDGES, D), BF),
        ((PICKS, D), BF),
        ((3, 2, UR, D), F32),
        ((2, UR, D), BF),
        ((2, UR, D), BF),
        ((2, 2, UR, D), BF),
        ((2, 2, UR, D), BF),
        ((UR, D), BF),
        ((UR, D), BF),
        ((4, IR, D), F32),
        ((4, 2, IR, D), F32),
        ((4, 2, IR, D), BF),
        ((4, 2, IR, D), BF),
        ((2, IR, D), BF),
        ((2, IR, D), BF),
        ((2, 2, IR, D), BF),
        ((2, 2, IR, D), BF),
        ((IR, D), BF),
        ((IR, D), BF),
    ]
    out = pl.pallas_call(
        kernel,
        out_shape=[
            jax.ShapeDtypeStruct((UR, D), F32),
            jax.ShapeDtypeStruct((1, UR), F32),
            jax.ShapeDtypeStruct((IR, D), F32),
            jax.ShapeDtypeStruct((1, IR), F32),
        ],
        in_specs=[vmem] * 7,
        out_specs=[vmem] * 4,
        scratch_shapes=[pltpu.VMEM(shape, kind) for shape, kind in scratch]
        + [pltpu.SemaphoreType.DMA((MESSAGES,)), pltpu.SemaphoreType.DMA((MESSAGES,))],
        compiler_params=pltpu.CompilerParams(
            collective_id=0, has_side_effects=True, vmem_limit_bytes=48 * 1024 * 1024
        ),
        name="step",
    )(
        user_table, user_state.reshape(1, UR), item_table, item_state.reshape(1, IR),
        edge_users, edge_items, negatives,
    )
    return (out[0], out[1].reshape(UR), out[2], out[3].reshape(IR))


def solution(mesh):
    in_specs = (
        P(("user", "item"), None),
        P(("user", "item")),
        P(("item", "user"), None),
        P(("item", "user")),
        P("user", "item", None),
        P("user", "item", None),
        P("item", None),
    )
    out_specs = (
        P(("user", "item"), None),
        P(("user", "item")),
        P(("item", "user"), None),
        P(("item", "user")),
    )
    return jax.shard_map(
        per_device, mesh=mesh, in_specs=in_specs, out_specs=out_specs, check_vma=False
    )
```

```python
import jax
import jax.numpy as jnp
from jax import lax
from jax.experimental import pallas as pl
from jax.experimental.pallas import tpu as pltpu
from jax.sharding import PartitionSpec as P

learn_rate = 0.1
MESH = pl.DeviceIdType.MESH
BF = jnp.bfloat16
F32 = jnp.float32

D = 256
EDGES = 2048
NEG = 1024
PICKS = EDGES + NEG
UR = 128
IR = 256
PLANE = 4 * IR
BLK = 512


def one_hot_cols(index, width):
    lane = lax.broadcasted_iota(jnp.int32, index.shape, 1)
    parts = [
        jnp.where(index == lane + 128 * c, F32(1), F32(0)).astype(BF) for c in range(width // 128)
    ]
    return jnp.concatenate(parts, axis=1)


def one_hot_rows(index, base, rows):
    row = lax.broadcasted_iota(jnp.int32, (rows, index.shape[1]), 0) + base
    return jnp.where(row == index, F32(1), F32(0)).astype(BF)


def to_column(row):
    return jnp.broadcast_to(row, (128, 128)).T


def adagrad(table, state_ref, total, out_ref, out_state_ref):
    rows = total.shape[0]
    mean = jnp.sum(total * total, axis=1, keepdims=True) * (1.0 / D)
    for b in range(rows // 128):
        part = slice(128 * b, 128 * (b + 1))
        new_state = to_column(state_ref[:, part]) + mean[part]
        out_state_ref[:, part] = new_state.T[0:1, :]
        scale = learn_rate / jnp.sqrt(new_state)
        out_ref[part, :] = table[part, :] - total[part] * jnp.concatenate([scale, scale], axis=1)


def kernel(
    user_table_h, user_state_h, item_table_h, item_state_h, edge_users_h, edge_items_h, negatives_h,
    new_user_table, new_user_state, new_item_table, new_item_state,
    user_table, user_state, item_table, item_state, edge_users, edge_items, negatives, load_sem,
    items, users, user_col, item_col, item_row, picked, picked_users, picked_negs, neg_grad,
    user_grad, item_grad,
    user_keep, u2s, u2r, uzs, uzr, uys, uyr,
    plane_sum, keep, sib_s, sib_r, z2s, z2r, zs, zr, ys, yr,
    send_sem, recv_sem,
):
    u, t = lax.axis_index("user"), lax.axis_index("item")
    k, yl, z = lax.rem(u, 2), lax.rem(lax.div(u, 2), 2), lax.div(u, 4)
    yh, x = lax.rem(t, 2), lax.div(t, 2)

    def user_id(zz, yy, kk):
        return (zz * 2 + yy) * 2 + kk

    def item_id(xx, yy):
        return xx * 2 + yy

    zp, zm, z2 = lax.rem(z + 1, 4), lax.rem(z + 3, 4), lax.rem(z + 2, 4)
    xp, xm, x2 = lax.rem(x + 1, 4), lax.rem(x + 3, 4), lax.rem(x + 2, 4)
    sib = {"user": user_id(z, yl, 1 - k)}
    yn = {"user": user_id(z, 1 - yl, k)}
    zup = {"user": user_id(zp, yl, k)}
    zdn = {"user": user_id(zm, yl, k)}
    hn = {"item": item_id(x, 1 - yh)}
    xup = {"item": item_id(xp, yh)}
    xdn = {"item": item_id(xm, yh)}

    pairs = (
        (item_table_h, item_table), (user_table_h, user_table), (edge_users_h, edge_users),
        (edge_items_h, edge_items), (negatives_h, negatives),
        (user_state_h, user_state), (item_state_h, item_state),
    )
    loads = [
        pltpu.make_async_copy(src, dst, load_sem.at[n]) for n, (src, dst) in enumerate(pairs)
    ]
    for load in loads:
        load.start()

    barrier = pltpu.get_barrier_semaphore()
    for peer in (sib, yn, zup, zdn, hn, xup, xdn):
        pl.semaphore_signal(barrier, inc=1, device_id=peer, device_id_type=MESH)

    copies = []

    def message(src, dst, peer):
        n = len(copies)
        copy = pltpu.make_async_remote_copy(
            src_ref=src, dst_ref=dst, send_sem=send_sem.at[n], recv_sem=recv_sem.at[n],
            device_id=peer, device_id_type=MESH,
        )
        copies.append(copy)
        return copy

    def send(src, dst, peer):
        copy = message(src, dst, peer)
        copy.start()
        return copy

    loads[0].wait()
    items[u] = item_table[...].astype(BF)
    loads[1].wait()
    users[t] = user_table[...].astype(BF)
    pl.semaphore_wait(barrier, 7)

    def slot(ref, s):
        return ref.at[s]

    own_i, own_u = slot(items, u), slot(users, t)
    m_zup = send(own_i, own_i, zup)
    m_zdn = send(own_i, own_i, zdn)
    m_yn = send(own_i, own_i, yn)
    m_sib = send(own_i, own_i, sib)
    m_xup = send(own_u, own_u, xup)
    m_xdn = send(own_u, own_u, xdn)
    m_hn = send(own_u, own_u, hn)

    for load in loads[2:]:
        load.wait()
    for b in range(EDGES // 128):
        part = slice(128 * b, 128 * (b + 1))
        user_col[part, :] = to_column(edge_users[0, :, part])
        item_col[part, :] = to_column(edge_items[0, :, part])
    for b in range(NEG // 128):
        item_col[EDGES + 128 * b:EDGES + 128 * (b + 1), :] = to_column(
            negatives[:, 128 * b:128 * (b + 1)]
        )
    item_row[:, :EDGES] = edge_items[0, :, :]
    item_row[:, EDGES:] = negatives[...]

    def pick_plane(zz, first):
        plane = items[pl.ds(zz * 4, 4)].reshape(PLANE, D)
        for b in range(PICKS // BLK):
            rows = pl.ds(b * BLK, BLK)
            one_hot = one_hot_cols(item_col[rows, :] - zz * PLANE, PLANE)
            got = jnp.dot(one_hot, plane, preferred_element_type=F32)
            picked[rows, :] = got if first else picked[rows, :] + got

    m_zup.wait_recv()
    s_zm = slot(items, user_id(zm, yl, k))
    lo, hi = pl.ds(0, IR // 2), pl.ds(IR // 2, IR // 2)
    m_z2a = send(s_zm.at[lo], s_zm.at[lo], zup)
    f_zm = send(s_zm, s_zm, sib)
    m_zdn.wait_recv()
    s_zp = slot(items, user_id(zp, yl, k))
    m_z2b = send(s_zp.at[hi], s_zp.at[hi], zdn)
    f_zp = send(s_zp, s_zp, sib)
    m_yn.wait_recv()
    s_yn = slot(items, user_id(z, 1 - yl, k))
    m_yzup = send(s_yn, s_yn, zup)
    m_yzdn = send(s_yn, s_yn, zdn)
    f_yn = send(s_yn, s_yn, sib)

    ulo, uhi = pl.ds(0, UR // 2), pl.ds(UR // 2, UR // 2)
    m_hn.wait_recv()
    s_hn = slot(users, item_id(x, 1 - yh))
    m_hxup = send(s_hn, s_hn, xup)
    m_hxdn = send(s_hn, s_hn, xdn)
    m_xup.wait_recv()
    s_xm = slot(users, item_id(xm, yh))
    m_x2a = send(s_xm.at[ulo], s_xm.at[ulo], xup)
    m_xdn.wait_recv()
    s_xp = slot(users, item_id(xp, yh))
    m_x2b = send(s_xp.at[uhi], s_xp.at[uhi], xdn)

    m_sib.wait_recv()
    f_yn.wait_recv()
    pick_plane(z, True)

    m_z2a.wait_recv()
    m_z2b.wait_recv()
    s_z2 = slot(items, user_id(z2, yl, k))
    m_z2y = send(s_z2, s_z2, yn)
    f_z2 = send(s_z2, s_z2, sib)
    m_hxup.wait_recv()
    s_hxm = slot(users, item_id(xm, 1 - yh))
    m_hx2a = send(s_hxm.at[ulo], s_hxm.at[ulo], xup)
    m_hxdn.wait_recv()
    s_hxp = slot(users, item_id(xp, 1 - yh))
    m_hx2b = send(s_hxp.at[uhi], s_hxp.at[uhi], xdn)

    m_yzup.wait_recv()
    s_yzm = slot(items, user_id(zm, 1 - yl, k))
    f_yzm = send(s_yzm, s_yzm, sib)
    m_yzdn.wait_recv()
    s_yzp = slot(items, user_id(zp, 1 - yl, k))
    f_yzp = send(s_yzp, s_yzp, sib)
    f_zm.wait_recv()
    f_yzm.wait_recv()
    pick_plane(zm, False)
    m_z2y.wait_recv()
    s_z2y = slot(items, user_id(z2, 1 - yl, k))
    f_z2y = send(s_z2y, s_z2y, sib)
    f_zp.wait_recv()
    f_yzp.wait_recv()
    pick_plane(zp, False)

    m_x2a.wait_recv()
    m_x2b.wait_recv()
    m_hx2a.wait_recv()
    m_hx2b.wait_recv()

    for b in range(EDGES // BLK):
        rows = pl.ds(b * BLK, BLK)
        one_hot = one_hot_cols(user_col[rows, :], 8 * UR)
        got = jnp.dot(one_hot, users[...].reshape(8 * UR, D), preferred_element_type=F32)
        picked_users[rows, :] = got.astype(BF)

    f_z2.wait_recv()
    f_z2y.wait_recv()
    pick_plane(z2, False)

    picked_negs[...] = picked[EDGES:, :].astype(BF)
    neg_grad[...] = jnp.zeros_like(neg_grad)

    for b in range(EDGES // BLK):
        rows = pl.ds(b * BLK, BLK)
        mine = picked_users[rows, :]
        wide = mine.astype(F32)
        item = picked[rows, :]
        negs = picked_negs[...]
        positive = jnp.sum(wide * item, axis=1, keepdims=True)
        pull = jax.nn.sigmoid(-positive)
        scores = lax.dot_general(mine, negs, (((1,), (1,)), ((), ())), preferred_element_type=F32)
        weights = (jax.nn.sigmoid(scores) * (1.0 / NEG)).astype(BF)
        user_grad[rows, :] = (
            -pull * item + jnp.dot(weights, negs, preferred_element_type=F32)
        ).astype(BF)
        item_grad[rows, :] = (-pull * wide).astype(BF)
        neg_grad[...] += lax.dot_general(
            weights, mine, (((0,), (0,)), ((), ())), preferred_element_type=F32
        )

    item_grad[EDGES:, :] = neg_grad[...].astype(BF)

    def spread_users(xx):
        one_hot = one_hot_rows(edge_users[0, :, :], xx * (2 * UR), 2 * UR)
        return jnp.dot(one_hot, user_grad[...], preferred_element_type=F32)

    got = spread_users(x2).astype(BF)
    u2s[...] = got.reshape(2, UR, D)
    m_u2p = send(u2s.at[0], u2r.at[0], xup)
    m_u2m = send(u2s.at[1], u2r.at[1], xdn)
    for n, xx in enumerate((xp, xm, x)):
        user_keep[n] = spread_users(xx).reshape(2, UR, D)

    def spread_items(zz, n):
        for m in range(4):
            one_hot = one_hot_rows(item_row[...], zz * PLANE + m * IR, IR)
            plane_sum[m] = jnp.dot(one_hot, item_grad[...], preferred_element_type=F32)
        for yy in range(2):
            sib_s[n, yy] = plane_sum[2 * yy + 1 - k].astype(BF)
            keep[n, yy] = plane_sum[2 * yy + k]
        return send(sib_s.at[n], sib_r.at[n], sib)

    m_s0 = spread_items(z2, 0)

    m_u2p.wait_recv()
    m_u2m.wait_recv()
    uzs[0, 0] = (user_keep[0, 0] + u2r[0].astype(F32)).astype(BF)
    uzs[0, 1] = user_keep[0, 1].astype(BF)
    m_uzp = send(uzs.at[0], uzr.at[0], xup)
    uzs[1, 0] = user_keep[1, 0].astype(BF)
    uzs[1, 1] = (user_keep[1, 1] + u2r[1].astype(F32)).astype(BF)
    m_uzm = send(uzs.at[1], uzr.at[1], xdn)

    m_s0.wait_recv()
    z2s[...] = (keep[0] + sib_r[0].astype(F32)).astype(BF)
    m_z2p = send(z2s.at[0], z2r.at[0], zup)
    m_z2m = send(z2s.at[1], z2r.at[1], zdn)

    m_s1 = spread_items(zp, 1)
    m_s2 = spread_items(zm, 2)

    m_s1.wait_recv()
    m_z2p.wait_recv()
    zs[0, 0] = (keep[1, 0] + sib_r[1, 0].astype(F32) + z2r[0].astype(F32)).astype(BF)
    zs[0, 1] = (keep[1, 1] + sib_r[1, 1].astype(F32)).astype(BF)
    m_zp = send(zs.at[0], zr.at[0], zup)
    m_s2.wait_recv()
    m_z2m.wait_recv()
    zs[1, 0] = (keep[2, 0] + sib_r[2, 0].astype(F32)).astype(BF)
    zs[1, 1] = (keep[2, 1] + sib_r[2, 1].astype(F32) + z2r[1].astype(F32)).astype(BF)
    m_zm = send(zs.at[1], zr.at[1], zdn)

    m_s3 = spread_items(z, 3)

    m_uzp.wait_recv()
    m_uzm.wait_recv()
    user_keep[2] = user_keep[2] + uzr[0].astype(F32) + uzr[1].astype(F32)
    uys[...] = user_keep[2, 1 - yh].astype(BF)
    m_uy = send(uys, uyr, hn)

    m_s3.wait_recv()
    keep[3] = keep[3] + sib_r[3].astype(F32)
    m_zp.wait_recv()
    m_zm.wait_recv()
    ys[...] = (keep[3, 1 - yl] + zr[0, 1 - yl].astype(F32) + zr[1, 1 - yl].astype(F32)).astype(BF)
    m_y = send(ys, yr, yn)
    keep[3, yl] = keep[3, yl] + zr[0, yl].astype(F32) + zr[1, yl].astype(F32)

    m_uy.wait_recv()
    adagrad(
        user_table, user_state, user_keep[2, yh] + uyr[...].astype(F32),
        new_user_table, new_user_state,
    )
    m_y.wait_recv()
    adagrad(
        item_table, item_state, keep[3, yl] + yr[...].astype(F32), new_item_table, new_item_state
    )
    for copy in copies:
        copy.wait_send()


MESSAGES = 40


def store(*refs):
    sources, targets, sem = refs[:4], refs[4:8], refs[8]
    moves = [
        pltpu.make_async_copy(a, b, sem.at[n]) for n, (a, b) in enumerate(zip(sources, targets))
    ]
    for move in moves:
        move.start()
    for move in moves:
        move.wait()


def per_device(user_table, user_state, item_table, item_state, edge_users, edge_items, negatives):
    vmem = pl.BlockSpec(memory_space=pltpu.VMEM)
    hbm = pl.BlockSpec(memory_space=pltpu.HBM)
    local = [
        ((UR, D), F32), ((1, UR), F32), ((IR, D), F32), ((1, IR), F32),
        ((1, 1, EDGES), jnp.int32), ((1, 1, EDGES), jnp.int32), ((1, NEG), jnp.int32),
    ]
    scratch = [
        ((16, IR, D), BF),
        ((8, UR, D), BF),
        ((EDGES, 128), jnp.int32),
        ((PICKS, 128), jnp.int32),
        ((1, PICKS), jnp.int32),
        ((PICKS, D), F32),
        ((EDGES, D), BF),
        ((NEG, D), BF),
        ((NEG, D), F32),
        ((EDGES, D), BF),
        ((PICKS, D), BF),
        ((3, 2, UR, D), F32),
        ((2, UR, D), BF),
        ((2, UR, D), BF),
        ((2, 2, UR, D), BF),
        ((2, 2, UR, D), BF),
        ((UR, D), BF),
        ((UR, D), BF),
        ((4, IR, D), F32),
        ((4, 2, IR, D), F32),
        ((4, 2, IR, D), BF),
        ((4, 2, IR, D), BF),
        ((2, IR, D), BF),
        ((2, IR, D), BF),
        ((2, 2, IR, D), BF),
        ((2, 2, IR, D), BF),
        ((IR, D), BF),
        ((IR, D), BF),
    ]
    shapes = [jax.ShapeDtypeStruct(shape, kind) for shape, kind in local[:4]]
    out = pl.pallas_call(
        kernel,
        out_shape=[pltpu.VMEM(shape, kind) for shape, kind in local[:4]],
        in_specs=[hbm] * 7,
        out_specs=[vmem] * 4,
        scratch_shapes=[pltpu.VMEM(shape, kind) for shape, kind in local]
        + [pltpu.SemaphoreType.DMA((7,))]
        + [pltpu.VMEM(shape, kind) for shape, kind in scratch]
        + [pltpu.SemaphoreType.DMA((MESSAGES,)), pltpu.SemaphoreType.DMA((MESSAGES,))],
        compiler_params=pltpu.CompilerParams(
            collective_id=0, has_side_effects=True, vmem_limit_bytes=48 * 1024 * 1024
        ),
        name="step",
    )(
        *(
            pltpu.with_memory_space_constraint(a, pltpu.HBM)
            for a in (
                user_table, user_state.reshape(1, UR), item_table, item_state.reshape(1, IR),
                edge_users, edge_items, negatives,
            )
        )
    )
    out = pl.pallas_call(
        store,
        out_shape=shapes,
        in_specs=[vmem] * 4,
        out_specs=[hbm] * 4,
        scratch_shapes=[pltpu.SemaphoreType.DMA((4,))],
        name="store",
    )(*out)
    return (out[0], out[1].reshape(UR), out[2], out[3].reshape(IR))


def solution(mesh):
    in_specs = (
        P(("user", "item"), None),
        P(("user", "item")),
        P(("item", "user"), None),
        P(("item", "user")),
        P("user", "item", None),
        P("user", "item", None),
        P("item", None),
    )
    out_specs = (
        P(("user", "item"), None),
        P(("user", "item")),
        P(("item", "user"), None),
        P(("item", "user")),
    )
    return jax.shard_map(
        per_device, mesh=mesh, in_specs=in_specs, out_specs=out_specs, check_vma=False
    )
```

```python
import jax
import jax.numpy as jnp
from jax import lax
from jax.experimental import pallas as pl
from jax.experimental.pallas import tpu as pltpu
from jax.sharding import PartitionSpec as P

learn_rate = 0.1
MESH = pl.DeviceIdType.MESH
BF = jnp.bfloat16
F32 = jnp.float32

D = 256
EDGES = 2048
NEG = 1024
PICKS = EDGES + NEG
UR = 128
IR = 256
PLANE = 4 * IR
BLK = 512


def one_hot_cols(index, width):
    lane = lax.broadcasted_iota(jnp.int32, index.shape, 1)
    parts = [
        jnp.where(index == lane + 128 * c, F32(1), F32(0)).astype(BF) for c in range(width // 128)
    ]
    return jnp.concatenate(parts, axis=1)


def one_hot_rows(index, base, rows):
    row = lax.broadcasted_iota(jnp.int32, (rows, index.shape[1]), 0) + base
    return jnp.where(row == index, F32(1), F32(0)).astype(BF)


def to_column(row):
    return jnp.broadcast_to(row, (128, 128)).T


def adagrad(table, state_ref, total, out_ref, out_state_ref):
    rows = total.shape[0]
    mean = jnp.sum(total * total, axis=1, keepdims=True) * (1.0 / D)
    for b in range(rows // 128):
        part = slice(128 * b, 128 * (b + 1))
        new_state = to_column(state_ref[:, part]) + mean[part]
        out_state_ref[:, part] = new_state.T[0:1, :]
        scale = learn_rate / jnp.sqrt(new_state)
        out_ref[part, :] = table[part, :] - total[part] * jnp.concatenate([scale, scale], axis=1)


def kernel(
    user_table_h, user_state_h, item_table_h, item_state_h, edge_users_h, edge_items_h, negatives_h,
    new_user_table, new_user_state, new_item_table, new_item_state,
    user_table, user_state, item_table, item_state, edge_users, edge_items, negatives, load_sem,
    items, users, turn, user_col, item_col, item_row, picked, picked_users, picked_negs, weights,
    user_grad, item_grad,
    user_keep, uxs, uxr, uys, uyr, keep, sib_s, sib_r, zs, zr,
    send_sem, recv_sem,
):
    u, t = lax.axis_index("user"), lax.axis_index("item")
    k, yl, z = lax.rem(u, 2), lax.rem(lax.div(u, 2), 2), lax.div(u, 4)
    yh, x = lax.rem(t, 2), lax.div(t, 2)
    ko, yo, ho = 1 - k, 1 - yl, 1 - yh
    zp, zm, z2 = lax.rem(z + 1, 4), lax.rem(z + 3, 4), lax.rem(z + 2, 4)
    xp, xm, x2 = lax.rem(x + 1, 4), lax.rem(x + 3, 4), lax.rem(x + 2, 4)

    def user_at(zz, yy, kk):
        return (zz * 2 + yy) * 2 + kk

    def user_peer(zz, yy, kk):
        return {"user": user_at(zz, yy, kk)}

    def item_peer(xx, yy):
        return {"item": xx * 2 + yy}

    sib, yn = user_peer(z, yl, ko), user_peer(z, yo, k)
    zup, zdn, zfar = user_peer(zp, yl, k), user_peer(zm, yl, k), user_peer(z2, yl, k)
    zup_o, zdn_o, zfar_o = user_peer(zp, yo, k), user_peer(zm, yo, k), user_peer(z2, yo, k)
    hn = item_peer(x, ho)
    xup, xdn, xfar = item_peer(xp, yh), item_peer(xm, yh), item_peer(x2, yh)
    peers = (sib, yn, zup, zdn, zfar, zup_o, zdn_o, zfar_o, hn, xup, xdn, xfar)

    barrier = pltpu.get_barrier_semaphore()
    for peer in peers:
        pl.semaphore_signal(barrier, inc=1, device_id=peer, device_id_type=MESH)

    pairs = (
        (item_table_h, item_table), (user_table_h, user_table), (edge_users_h, edge_users),
        (edge_items_h, edge_items), (negatives_h, negatives),
        (user_state_h, user_state), (item_state_h, item_state),
    )
    loads = [
        pltpu.make_async_copy(src, dst, load_sem.at[n]) for n, (src, dst) in enumerate(pairs)
    ]
    for load in loads:
        load.start()

    step = pl.when(u >= 0)

    copies = []

    def send(src, dst, peer):
        n = len(copies)
        copy = pltpu.make_async_remote_copy(
            src_ref=src, dst_ref=dst, send_sem=send_sem.at[n], recv_sem=recv_sem.at[n],
            device_id=peer, device_id_type=MESH,
        )
        copies.append(copy)
        copy.start()
        return copy

    def share(ref, peer):
        return send(ref, ref, peer)

    loads[0].wait()
    items[u] = item_table[...].astype(BF)
    loads[1].wait()
    users[t] = user_table[...].astype(BF)
    pl.semaphore_wait(barrier, len(peers))

    own_i, own_u = items.at[u], users.at[t]
    m_sib = share(own_i, sib)
    m_yn = share(own_i, yn)
    m_far = share(own_i, zfar)
    m_up = share(own_i, zup)
    m_dn = share(own_i, zdn)
    m_hn = share(own_u, hn)
    m_xup = share(own_u, xup)
    m_xdn = share(own_u, xdn)
    m_xfar = share(own_u, xfar)

    for load in loads[2:]:
        load.wait()
    @step
    def _():
        turn[...] = jnp.zeros_like(turn)
        item_tiles, neg_tiles = EDGES // 128, NEG // 128
        for b in range(item_tiles):
            part = slice(128 * b, 128 * (b + 1))
            turn[b:b + 1, :] = edge_items[0, :, part]
            turn[item_tiles + neg_tiles + b:item_tiles + neg_tiles + b + 1, :] = edge_users[0, :, part]
        for b in range(neg_tiles):
            turn[item_tiles + b:item_tiles + b + 1, :] = negatives[:, 128 * b:128 * (b + 1)]
        turned = turn[...].T
        for b in range(item_tiles + neg_tiles):
            item_col[128 * b:128 * (b + 1), :] = jnp.broadcast_to(turned[:, b:b + 1], (128, 128))
        for b in range(item_tiles):
            c = item_tiles + neg_tiles + b
            user_col[128 * b:128 * (b + 1), :] = jnp.broadcast_to(turned[:, c:c + 1], (128, 128))
        item_row[:, :EDGES] = edge_items[0, :, :]
        item_row[:, EDGES:] = negatives[...]

    def pick_half(zz, yy, first=False):
        @step
        def _():
            place = zz * 2 + yy
            half = items[pl.ds(place * 2, 2)].reshape(2 * IR, D)
            for b in range(PICKS // BLK):
                rows = pl.ds(b * BLK, BLK)
                one_hot = one_hot_cols(item_col[rows, :] - place * (2 * IR), 2 * IR)
                got = jnp.dot(one_hot, half, preferred_element_type=F32)
                picked[rows, :] = got if first else picked[rows, :] + got

    def item_shard(zz, yy):
        return items.at[user_at(zz, yy, k)]

    m_sib.wait_recv()
    pick_half(z, yl, True)

    m_yn.wait_recv()
    m_yup = share(item_shard(z, yo), zup)
    m_ydn = share(item_shard(z, yo), zdn)
    f_yn = share(item_shard(z, yo), sib)
    m_hn.wait_recv()
    near = users.at[x * 2 + ho]
    m_hup = share(near, xup)
    m_hdn = share(near, xdn)
    m_hfar = share(near, xfar)
    m_far.wait_recv()
    m_fary = share(item_shard(z2, yl), yn)
    f_far = share(item_shard(z2, yl), sib)
    m_up.wait_recv()
    f_dn = share(item_shard(zm, yl), sib)
    m_dn.wait_recv()
    f_up = share(item_shard(zp, yl), sib)

    f_yn.wait_recv()
    pick_half(z, yo)
    f_far.wait_recv()
    pick_half(z2, yl)
    f_dn.wait_recv()
    pick_half(zm, yl)
    m_yup.wait_recv()
    f_ydn = share(item_shard(zm, yo), sib)
    m_ydn.wait_recv()
    f_yup = share(item_shard(zp, yo), sib)
    f_up.wait_recv()
    pick_half(zp, yl)

    for copy in (m_xup, m_xdn, m_xfar, m_hup, m_hdn, m_hfar):
        copy.wait_recv()
    @step
    def _():
        for b in range(EDGES // BLK):
            rows = pl.ds(b * BLK, BLK)
            one_hot = one_hot_cols(user_col[rows, :], 8 * UR)
            got = jnp.dot(one_hot, users[...].reshape(8 * UR, D), preferred_element_type=F32)
            picked_users[rows, :] = got.astype(BF)

    m_fary.wait_recv()
    f_fary = share(item_shard(z2, yo), sib)
    f_ydn.wait_recv()
    pick_half(zm, yo)
    f_yup.wait_recv()
    pick_half(zp, yo)
    f_fary.wait_recv()
    pick_half(z2, yo)

    @step
    def _():
        picked_negs[...] = picked[EDGES:, :].astype(BF)
        for b in range(EDGES // BLK):
            rows = pl.ds(b * BLK, BLK)
            mine = picked_users[rows, :]
            wide = mine.astype(F32)
            item = picked[rows, :]
            scores = lax.dot_general(
                mine, picked_negs[...], (((1,), (1,)), ((), ())), preferred_element_type=F32
            )
            weights[rows, :] = (jax.nn.sigmoid(scores) * (1.0 / NEG)).astype(BF)
            positive = jnp.sum(wide * item, axis=1, keepdims=True)
            pull = jax.nn.sigmoid(-positive)
            picked[rows, :] = -pull * item
            item_grad[rows, :] = (-pull * wide).astype(BF)
        item_grad[EDGES:, :] = lax.dot_general(
            weights[...], picked_users[...], (((0,), (0,)), ((), ())), preferred_element_type=F32
        ).astype(BF)

    def spread_items(zz, yy, kk):
        one_hot = one_hot_rows(item_row[...], user_at(zz, yy, kk) * IR, IR)
        return jnp.dot(one_hot, item_grad[...], preferred_element_type=F32)

    def for_sib(n, places):
        @step
        def _():
            for m, (zz, yy) in enumerate(places):
                sib_s[n, m] = spread_items(zz, yy, ko).astype(BF)

        return send(sib_s.at[n], sib_r.at[n], sib)

    def for_core(n, places):
        @step
        def _():
            for m, (zz, yy) in enumerate(places):
                keep[n, m] = spread_items(zz, yy, k)

    def to_owners(n, copy, peers):
        copy.wait_recv()

        @step
        def _():
            for m in range(len(peers)):
                zs[n, m] = (keep[n, m] + sib_r[n, m].astype(F32)).astype(BF)

        return [send(zs.at[n, m], zr.at[n, m], peer) for m, peer in enumerate(peers)]

    far_two = ((z2, yl), (z2, yo))
    c0 = for_sib(0, far_two)
    for_core(0, far_two)
    o0 = to_owners(0, c0, (zfar, zfar_o))

    @step
    def _():
        for b in range(EDGES // BLK):
            rows = pl.ds(b * BLK, BLK)
            user_grad[rows, :] = (
                picked[rows, :]
                + jnp.dot(weights[rows, :], picked_negs[...], preferred_element_type=F32)
            ).astype(BF)

    def spread_users(xx):
        one_hot = one_hot_rows(edge_users[0, :, :], xx * (2 * UR), 2 * UR)
        got = jnp.dot(one_hot, user_grad[...], preferred_element_type=F32)
        return got.reshape(2, UR, D)

    x_copies = []
    for n, (xx, peer) in enumerate(((x2, xfar), (xp, xup), (xm, xdn))):
        @step
        def _():
            uxs[n] = spread_users(xx).astype(BF)

        x_copies.append(send(uxs.at[n], uxr.at[n], peer))

    @step
    def _():
        user_keep[...] = spread_users(x)


    other_two = ((zp, yo), (zm, yo))
    c1 = for_sib(1, other_two)
    for_core(1, other_two)
    o1 = to_owners(1, c1, (zup_o, zdn_o))
    same_two = ((zp, yl), (zm, yl))
    c2 = for_sib(2, same_two)
    for_core(2, same_two)
    own_two = ((z, yo), (z, yl))
    c3 = for_sib(3, own_two)
    o2 = to_owners(2, c2, (zup, zdn))
    for_core(3, own_two)
    o3 = to_owners(3, c3, (yn,))

    for copy in x_copies:
        copy.wait_recv()
    @step
    def _():
        uys[...] = (
            user_keep[ho] + uxr[0, ho].astype(F32) + uxr[1, ho].astype(F32) + uxr[2, ho].astype(F32)
        ).astype(BF)

    m_uy = send(uys, uyr, hn)

    m_uy.wait_recv()
    user_total = (
        user_keep[yh] + uxr[0, yh].astype(F32) + uxr[1, yh].astype(F32) + uxr[2, yh].astype(F32)
        + uyr[...].astype(F32)
    )
    adagrad(user_table, user_state, user_total, new_user_table, new_user_state)

    item_total = keep[3, 1] + sib_r[3, 1].astype(F32)
    for n, sent in enumerate((o0, o1, o2, o3)):
        for m, copy in enumerate(sent):
            copy.wait_recv()
            item_total = item_total + zr[n, m].astype(F32)
    adagrad(item_table, item_state, item_total, new_item_table, new_item_state)
    for copy in copies:
        copy.wait_send()


MESSAGES = 40


def store(*refs):
    sources, targets, sem = refs[:4], refs[4:8], refs[8]
    moves = [
        pltpu.make_async_copy(a, b, sem.at[n]) for n, (a, b) in enumerate(zip(sources, targets))
    ]
    for move in moves:
        move.start()
    for move in moves:
        move.wait()


def per_device(user_table, user_state, item_table, item_state, edge_users, edge_items, negatives):
    vmem = pl.BlockSpec(memory_space=pltpu.VMEM)
    hbm = pl.BlockSpec(memory_space=pltpu.HBM)
    local = [
        ((UR, D), F32), ((1, UR), F32), ((IR, D), F32), ((1, IR), F32),
        ((1, 1, EDGES), jnp.int32), ((1, 1, EDGES), jnp.int32), ((1, NEG), jnp.int32),
    ]
    scratch = [
        ((16, IR, D), BF),
        ((8, UR, D), BF),
        ((128, 128), jnp.int32),
        ((EDGES, 128), jnp.int32),
        ((PICKS, 128), jnp.int32),
        ((1, PICKS), jnp.int32),
        ((PICKS, D), F32),
        ((EDGES, D), BF),
        ((NEG, D), BF),
        ((EDGES, NEG), BF),
        ((EDGES, D), BF),
        ((PICKS, D), BF),
        ((2, UR, D), F32),
        ((3, 2, UR, D), BF),
        ((3, 2, UR, D), BF),
        ((UR, D), BF),
        ((UR, D), BF),
        ((4, 2, IR, D), F32),
        ((4, 2, IR, D), BF),
        ((4, 2, IR, D), BF),
        ((4, 2, IR, D), BF),
        ((4, 2, IR, D), BF),
    ]
    shapes = [jax.ShapeDtypeStruct(shape, kind) for shape, kind in local[:4]]
    out = pl.pallas_call(
        kernel,
        out_shape=[pltpu.VMEM(shape, kind) for shape, kind in local[:4]],
        in_specs=[hbm] * 7,
        out_specs=[vmem] * 4,
        scratch_shapes=[pltpu.VMEM(shape, kind) for shape, kind in local]
        + [pltpu.SemaphoreType.DMA((7,))]
        + [pltpu.VMEM(shape, kind) for shape, kind in scratch]
        + [pltpu.SemaphoreType.DMA((MESSAGES,)), pltpu.SemaphoreType.DMA((MESSAGES,))],
        compiler_params=pltpu.CompilerParams(
            collective_id=0, has_side_effects=True, vmem_limit_bytes=48 * 1024 * 1024
        ),
        name="step",
    )(
        *(
            pltpu.with_memory_space_constraint(a, pltpu.HBM)
            for a in (
                user_table, user_state.reshape(1, UR), item_table, item_state.reshape(1, IR),
                edge_users, edge_items, negatives,
            )
        )
    )
    out = pl.pallas_call(
        store,
        out_shape=shapes,
        in_specs=[vmem] * 4,
        out_specs=[hbm] * 4,
        scratch_shapes=[pltpu.SemaphoreType.DMA((4,))],
        compiler_params=pltpu.CompilerParams(vmem_limit_bytes=16 * 1024 * 1024),
        name="store",
    )(*(pltpu.with_memory_space_constraint(a, pltpu.VMEM) for a in out))
    return (out[0], out[1].reshape(UR), out[2], out[3].reshape(IR))


def solution(mesh):
    in_specs = (
        P(("user", "item"), None),
        P(("user", "item")),
        P(("item", "user"), None),
        P(("item", "user")),
        P("user", "item", None),
        P("user", "item", None),
        P("item", None),
    )
    out_specs = (
        P(("user", "item"), None),
        P(("user", "item")),
        P(("item", "user"), None),
        P(("item", "user")),
    )
    return jax.shard_map(
        per_device, mesh=mesh, in_specs=in_specs, out_specs=out_specs, check_vma=False
    )
```

```python
import jax
import jax.numpy as jnp
from jax import lax
from jax.experimental import pallas as pl
from jax.experimental.pallas import tpu as pltpu
from jax.sharding import PartitionSpec as P

learn_rate = 0.1
MESH = pl.DeviceIdType.MESH
BF = jnp.bfloat16
F32 = jnp.float32

D = 256
EDGES = 2048
NEG = 1024
PICKS = EDGES + NEG
UR = 128
IR = 256
PLANE = 4 * IR
BLK = 512


def one_hot_cols(index, width):
    lane = lax.broadcasted_iota(jnp.int32, index.shape, 1)
    parts = [
        jnp.where(index == lane + 128 * c, F32(1), F32(0)).astype(BF) for c in range(width // 128)
    ]
    return jnp.concatenate(parts, axis=1)


def one_hot_rows(index, base, rows):
    row = lax.broadcasted_iota(jnp.int32, (rows, index.shape[1]), 0) + base
    return jnp.where(row == index, F32(1), F32(0)).astype(BF)


def to_column(row):
    return jnp.broadcast_to(row, (128, 128)).T


def adagrad(table, state_ref, total, out_ref, out_state_ref):
    rows = total.shape[0]
    mean = jnp.sum(total * total, axis=1, keepdims=True) * (1.0 / D)
    for b in range(rows // 128):
        part = slice(128 * b, 128 * (b + 1))
        new_state = to_column(state_ref[:, part]) + mean[part]
        out_state_ref[:, part] = new_state.T[0:1, :]
        scale = learn_rate / jnp.sqrt(new_state)
        out_ref[part, :] = table[part, :] - total[part] * jnp.concatenate([scale, scale], axis=1)


def kernel(
    user_table_h, user_state_h, item_table_h, item_state_h, edge_users_h, edge_items_h, negatives_h,
    new_user_table, new_user_state, new_item_table, new_item_state,
    user_table, user_state, item_table, item_state, edge_users, edge_items, negatives, load_sem,
    items, users, turn, user_col, item_col, item_row, picked, picked_users, picked_negs, weights,
    user_grad, item_grad,
    user_keep, uxs, uxr, uys, uyr, keep, sib_s, sib_r, zs, zr,
    send_sem, recv_sem,
):
    u, t = lax.axis_index("user"), lax.axis_index("item")
    k, yl, z = lax.rem(u, 2), lax.rem(lax.div(u, 2), 2), lax.div(u, 4)
    yh, x = lax.rem(t, 2), lax.div(t, 2)
    ko, yo, ho = 1 - k, 1 - yl, 1 - yh
    zp, zm, z2 = lax.rem(z + 1, 4), lax.rem(z + 3, 4), lax.rem(z + 2, 4)
    xp, xm, x2 = lax.rem(x + 1, 4), lax.rem(x + 3, 4), lax.rem(x + 2, 4)

    def user_at(zz, yy, kk):
        return (zz * 2 + yy) * 2 + kk

    def user_peer(zz, yy, kk):
        return {"user": user_at(zz, yy, kk)}

    def item_peer(xx, yy):
        return {"item": xx * 2 + yy}

    sib, yn = user_peer(z, yl, ko), user_peer(z, yo, k)
    zup, zdn, zfar = user_peer(zp, yl, k), user_peer(zm, yl, k), user_peer(z2, yl, k)
    zup_o, zdn_o = user_peer(zp, yo, k), user_peer(zm, yo, k)
    hn = item_peer(x, ho)
    xup, xdn, xfar = item_peer(xp, yh), item_peer(xm, yh), item_peer(x2, yh)
    peers = (sib, yn, zup, zdn, zfar, zup_o, zdn_o, hn, xup, xdn, xfar)

    barrier = pltpu.get_barrier_semaphore()
    for peer in peers:
        pl.semaphore_signal(barrier, inc=1, device_id=peer, device_id_type=MESH)

    pairs = (
        (item_table_h, item_table), (user_table_h, user_table), (edge_users_h, edge_users),
        (edge_items_h, edge_items), (negatives_h, negatives),
        (user_state_h, user_state), (item_state_h, item_state),
    )
    loads = [
        pltpu.make_async_copy(src, dst, load_sem.at[n]) for n, (src, dst) in enumerate(pairs)
    ]
    for load in loads:
        load.start()

    step = pl.when(u >= 0)

    copies = []

    def send(src, dst, peer):
        n = len(copies)
        copy = pltpu.make_async_remote_copy(
            src_ref=src, dst_ref=dst, send_sem=send_sem.at[n], recv_sem=recv_sem.at[n],
            device_id=peer, device_id_type=MESH,
        )
        copies.append(copy)
        copy.start()
        return copy

    def share(ref, peer):
        return send(ref, ref, peer)

    loads[0].wait()
    items[u] = item_table[...].astype(BF)
    loads[1].wait()
    users[t] = user_table[...].astype(BF)
    pl.semaphore_wait(barrier, len(peers))

    own_i, own_u = items.at[u], users.at[t]
    m_sib = share(own_i, sib)
    m_yn = share(own_i, yn)
    m_far = share(own_i, zfar)
    m_up = share(own_i, zup)
    m_dn = share(own_i, zdn)
    m_hn = share(own_u, hn)
    m_xup = share(own_u, xup)
    m_xdn = share(own_u, xdn)
    m_xfar = share(own_u, xfar)

    for load in loads[2:]:
        load.wait()
    @step
    def _():
        turn[...] = jnp.zeros_like(turn)
        item_tiles, neg_tiles = EDGES // 128, NEG // 128
        for b in range(item_tiles):
            part = slice(128 * b, 128 * (b + 1))
            turn[b:b + 1, :] = edge_items[0, :, part]
            turn[item_tiles + neg_tiles + b:item_tiles + neg_tiles + b + 1, :] = edge_users[0, :, part]
        for b in range(neg_tiles):
            turn[item_tiles + b:item_tiles + b + 1, :] = negatives[:, 128 * b:128 * (b + 1)]
        turned = turn[...].T
        for b in range(item_tiles + neg_tiles):
            item_col[128 * b:128 * (b + 1), :] = jnp.broadcast_to(turned[:, b:b + 1], (128, 128))
        for b in range(item_tiles):
            c = item_tiles + neg_tiles + b
            user_col[128 * b:128 * (b + 1), :] = jnp.broadcast_to(turned[:, c:c + 1], (128, 128))
        item_row[:, :EDGES] = edge_items[0, :, :]
        item_row[:, EDGES:] = negatives[...]

    def pick_half(zz, yy, first=False):
        @step
        def _():
            place = zz * 2 + yy
            half = items[pl.ds(place * 2, 2)].reshape(2 * IR, D)
            for b in range(PICKS // BLK):
                rows = pl.ds(b * BLK, BLK)
                one_hot = one_hot_cols(item_col[rows, :] - place * (2 * IR), 2 * IR)
                got = jnp.dot(one_hot, half, preferred_element_type=F32)
                picked[rows, :] = got if first else picked[rows, :] + got

    def item_shard(zz, yy):
        return items.at[user_at(zz, yy, k)]

    m_sib.wait_recv()
    pick_half(z, yl, True)

    m_yn.wait_recv()
    m_yup = share(item_shard(z, yo), zup)
    m_ydn = share(item_shard(z, yo), zdn)
    f_yn = share(item_shard(z, yo), sib)
    m_hn.wait_recv()
    near = users.at[x * 2 + ho]
    m_hup = share(near, xup)
    m_hdn = share(near, xdn)
    m_hfar = share(near, xfar)
    m_far.wait_recv()
    m_fary = share(item_shard(z2, yl), yn)
    f_far = share(item_shard(z2, yl), sib)
    m_up.wait_recv()
    f_dn = share(item_shard(zm, yl), sib)
    m_dn.wait_recv()
    f_up = share(item_shard(zp, yl), sib)

    f_yn.wait_recv()
    pick_half(z, yo)
    f_far.wait_recv()
    pick_half(z2, yl)
    f_dn.wait_recv()
    pick_half(zm, yl)
    m_yup.wait_recv()
    f_ydn = share(item_shard(zm, yo), sib)
    m_ydn.wait_recv()
    f_yup = share(item_shard(zp, yo), sib)
    f_up.wait_recv()
    pick_half(zp, yl)

    for copy in (m_xup, m_xdn, m_xfar, m_hup, m_hdn, m_hfar):
        copy.wait_recv()
    @step
    def _():
        for b in range(EDGES // BLK):
            rows = pl.ds(b * BLK, BLK)
            one_hot = one_hot_cols(user_col[rows, :], 8 * UR)
            got = jnp.dot(one_hot, users[...].reshape(8 * UR, D), preferred_element_type=F32)
            picked_users[rows, :] = got.astype(BF)

    m_fary.wait_recv()
    f_fary = share(item_shard(z2, yo), sib)
    f_ydn.wait_recv()
    pick_half(zm, yo)
    f_yup.wait_recv()
    pick_half(zp, yo)
    f_fary.wait_recv()
    pick_half(z2, yo)

    @step
    def _():
        picked_negs[...] = picked[EDGES:, :].astype(BF)
        for b in range(EDGES // BLK):
            rows = pl.ds(b * BLK, BLK)
            mine = picked_users[rows, :]
            wide = mine.astype(F32)
            item = picked[rows, :]
            scores = lax.dot_general(
                mine, picked_negs[...], (((1,), (1,)), ((), ())), preferred_element_type=F32
            )
            weights[rows, :] = (jax.nn.sigmoid(scores) * (1.0 / NEG)).astype(BF)
            positive = jnp.sum(wide * item, axis=1, keepdims=True)
            pull = jax.nn.sigmoid(-positive)
            picked[rows, :] = -pull * item
            item_grad[rows, :] = (-pull * wide).astype(BF)
        item_grad[EDGES:, :] = lax.dot_general(
            weights[...], picked_users[...], (((0,), (0,)), ((), ())), preferred_element_type=F32
        ).astype(BF)

    def spread_items(zz, yy, kk):
        one_hot = one_hot_rows(item_row[...], user_at(zz, yy, kk) * IR, IR)
        return jnp.dot(one_hot, item_grad[...], preferred_element_type=F32)

    def for_sib(n, places):
        @step
        def _():
            for m, (zz, yy) in enumerate(places):
                sib_s[n, m] = spread_items(zz, yy, ko).astype(BF)

        several = pl.ds(0, len(places))
        return send(sib_s.at[n, several], sib_r.at[n, several], sib)

    def for_core(n, places):
        @step
        def _():
            for m, (zz, yy) in enumerate(places):
                keep[n, m] = spread_items(zz, yy, k)

    def to_owners(n, copy, peers, joined=False):
        copy.wait_recv()

        @step
        def _():
            for m in range(len(peers)):
                total = keep[n, m] + sib_r[n, m].astype(F32)
                if joined:
                    total = total + zr[0, m].astype(F32)
                zs[n, m] = total.astype(BF)

        return [send(zs.at[n, m], zr.at[n, m], peer) for m, peer in enumerate(peers)]

    first = ((z2, yl), (z2, yo), (z, yo))
    c0 = for_sib(0, first)
    for_core(0, first)
    o0 = to_owners(0, c0, (zup, zdn, yn))

    @step
    def _():
        for b in range(EDGES // BLK):
            rows = pl.ds(b * BLK, BLK)
            user_grad[rows, :] = (
                picked[rows, :]
                + jnp.dot(weights[rows, :], picked_negs[...], preferred_element_type=F32)
            ).astype(BF)

    def spread_users(xx):
        one_hot = one_hot_rows(edge_users[0, :, :], xx * (2 * UR), 2 * UR)
        got = jnp.dot(one_hot, user_grad[...], preferred_element_type=F32)
        return got.reshape(2, UR, D)

    x_copies, x_same = [], []
    for n, (xx, peer) in enumerate(((x2, xfar), (xp, xup), (xm, xdn))):
        @step
        def _():
            uxs[n] = spread_users(xx).astype(BF)

        x_copies.append(send(uxs.at[n, ho], uxr.at[n, ho], peer))
        x_same.append((n, peer))

    @step
    def _():
        user_keep[...] = spread_users(x)


    x_same = [send(uxs.at[n, yh], uxr.at[n, yh], peer) for n, peer in x_same]
    alone_two = ((zp, yo), (zm, yl))
    c1 = for_sib(1, alone_two)
    for_core(1, alone_two)
    o1 = to_owners(1, c1, (zup_o, zdn))
    joined_two = ((zp, yl), (zm, yo))
    c2 = for_sib(2, joined_two)
    for_core(2, joined_two)
    o0[0].wait_recv()
    o0[1].wait_recv()
    o2 = to_owners(2, c2, (zup, zdn_o), True)
    c3 = for_sib(3, ((z, yl),))

    for copy in x_copies:
        copy.wait_recv()
    @step
    def _():
        uys[...] = (
            user_keep[ho] + uxr[0, ho].astype(F32) + uxr[1, ho].astype(F32) + uxr[2, ho].astype(F32)
        ).astype(BF)

    m_uy = send(uys, uyr, hn)
    for_core(3, ((z, yl),))
    for copy in x_same:
        copy.wait_recv()

    m_uy.wait_recv()
    user_total = (
        user_keep[yh] + uxr[0, yh].astype(F32) + uxr[1, yh].astype(F32) + uxr[2, yh].astype(F32)
        + uyr[...].astype(F32)
    )
    adagrad(user_table, user_state, user_total, new_user_table, new_user_state)

    c3.wait_recv()
    item_total = keep[3, 0] + sib_r[3, 0].astype(F32)
    arrivals = ((0, 2, o0[2]), (1, 0, o1[0]), (1, 1, o1[1]), (2, 0, o2[0]), (2, 1, o2[1]))
    for n, m, copy in arrivals:
        copy.wait_recv()
        item_total = item_total + zr[n, m].astype(F32)
    adagrad(item_table, item_state, item_total, new_item_table, new_item_state)
    for copy in copies:
        copy.wait_send()


MESSAGES = 40


def store(*refs):
    sources, targets, sem = refs[:4], refs[4:8], refs[8]
    moves = [
        pltpu.make_async_copy(a, b, sem.at[n]) for n, (a, b) in enumerate(zip(sources, targets))
    ]
    for move in moves:
        move.start()
    for move in moves:
        move.wait()


def per_device(user_table, user_state, item_table, item_state, edge_users, edge_items, negatives):
    vmem = pl.BlockSpec(memory_space=pltpu.VMEM)
    hbm = pl.BlockSpec(memory_space=pltpu.HBM)
    local = [
        ((UR, D), F32), ((1, UR), F32), ((IR, D), F32), ((1, IR), F32),
        ((1, 1, EDGES), jnp.int32), ((1, 1, EDGES), jnp.int32), ((1, NEG), jnp.int32),
    ]
    scratch = [
        ((16, IR, D), BF),
        ((8, UR, D), BF),
        ((128, 128), jnp.int32),
        ((EDGES, 128), jnp.int32),
        ((PICKS, 128), jnp.int32),
        ((1, PICKS), jnp.int32),
        ((PICKS, D), F32),
        ((EDGES, D), BF),
        ((NEG, D), BF),
        ((EDGES, NEG), BF),
        ((EDGES, D), BF),
        ((PICKS, D), BF),
        ((2, UR, D), F32),
        ((3, 2, UR, D), BF),
        ((3, 2, UR, D), BF),
        ((UR, D), BF),
        ((UR, D), BF),
        ((4, 3, IR, D), F32),
        ((4, 3, IR, D), BF),
        ((4, 3, IR, D), BF),
        ((4, 3, IR, D), BF),
        ((4, 3, IR, D), BF),
    ]
    shapes = [jax.ShapeDtypeStruct(shape, kind) for shape, kind in local[:4]]
    out = pl.pallas_call(
        kernel,
        out_shape=[pltpu.VMEM(shape, kind) for shape, kind in local[:4]],
        in_specs=[hbm] * 7,
        out_specs=[vmem] * 4,
        scratch_shapes=[pltpu.VMEM(shape, kind) for shape, kind in local]
        + [pltpu.SemaphoreType.DMA((7,))]
        + [pltpu.VMEM(shape, kind) for shape, kind in scratch]
        + [pltpu.SemaphoreType.DMA((MESSAGES,)), pltpu.SemaphoreType.DMA((MESSAGES,))],
        compiler_params=pltpu.CompilerParams(
            collective_id=0, has_side_effects=True, vmem_limit_bytes=48 * 1024 * 1024
        ),
        name="step",
    )(
        *(
            pltpu.with_memory_space_constraint(a, pltpu.HBM)
            for a in (
                user_table, user_state.reshape(1, UR), item_table, item_state.reshape(1, IR),
                edge_users, edge_items, negatives,
            )
        )
    )
    out = pl.pallas_call(
        store,
        out_shape=shapes,
        in_specs=[vmem] * 4,
        out_specs=[hbm] * 4,
        scratch_shapes=[pltpu.SemaphoreType.DMA((4,))],
        compiler_params=pltpu.CompilerParams(vmem_limit_bytes=16 * 1024 * 1024),
        name="store",
    )(*(pltpu.with_memory_space_constraint(a, pltpu.VMEM) for a in out))
    return (out[0], out[1].reshape(UR), out[2], out[3].reshape(IR))


def solution(mesh):
    in_specs = (
        P(("user", "item"), None),
        P(("user", "item")),
        P(("item", "user"), None),
        P(("item", "user")),
        P("user", "item", None),
        P("user", "item", None),
        P("item", None),
    )
    out_specs = (
        P(("user", "item"), None),
        P(("user", "item")),
        P(("item", "user"), None),
        P(("item", "user")),
    )
    return jax.shard_map(
        per_device, mesh=mesh, in_specs=in_specs, out_specs=out_specs, check_vma=False
    )
```

```python
import jax
import jax.numpy as jnp
from jax import lax
from jax.experimental import pallas as pl
from jax.experimental.pallas import tpu as pltpu
from jax.sharding import PartitionSpec as P

learn_rate = 0.1
MESH = pl.DeviceIdType.MESH
BF = jnp.bfloat16
F32 = jnp.float32

D = 256
EDGES = 2048
NEG = 1024
PICKS = EDGES + NEG
UR = 128
IR = 256
PLANE = 4 * IR
BLK = 512


def one_hot_cols(index, width):
    lane = lax.broadcasted_iota(jnp.int32, index.shape, 1)
    parts = [
        jnp.where(index == lane + 128 * c, F32(1), F32(0)).astype(BF) for c in range(width // 128)
    ]
    return jnp.concatenate(parts, axis=1)


def one_hot_rows(index, base, rows):
    row = lax.broadcasted_iota(jnp.int32, (rows, index.shape[1]), 0) + base
    return jnp.where(row == index, F32(1), F32(0)).astype(BF)


def to_column(row):
    return jnp.broadcast_to(row, (128, 128)).T


def adagrad(table, state_ref, total, out_ref, out_state_ref):
    rows = total.shape[0]
    mean = jnp.sum(total * total, axis=1, keepdims=True) * (1.0 / D)
    for b in range(rows // 128):
        part = slice(128 * b, 128 * (b + 1))
        new_state = to_column(state_ref[:, part]) + mean[part]
        out_state_ref[:, part] = new_state.T[0:1, :]
        scale = learn_rate / jnp.sqrt(new_state)
        out_ref[part, :] = table[part, :] - total[part] * jnp.concatenate([scale, scale], axis=1)


def kernel(
    user_table_h, user_state_h, item_table_h, item_state_h, edge_users_h, edge_items_h, negatives_h,
    new_user_table, new_user_state, new_item_table, new_item_state,
    user_table, user_state, item_table, item_state, edge_users, edge_items, negatives, load_sem,
    items, users, turn, user_col, item_col, item_row, picked, picked_users, picked_negs, weights,
    user_grad, item_grad,
    user_keep, uxs, uxr, uys, uyr, keep, sib_s, sib_r, zs, zr,
    send_sem, recv_sem,
):
    u, t = lax.axis_index("user"), lax.axis_index("item")
    k, yl, z = lax.rem(u, 2), lax.rem(lax.div(u, 2), 2), lax.div(u, 4)
    yh, x = lax.rem(t, 2), lax.div(t, 2)
    ko, yo, ho = 1 - k, 1 - yl, 1 - yh
    zp, zm, z2 = lax.rem(z + 1, 4), lax.rem(z + 3, 4), lax.rem(z + 2, 4)
    xp, xm, x2 = lax.rem(x + 1, 4), lax.rem(x + 3, 4), lax.rem(x + 2, 4)

    def user_at(zz, yy, kk):
        return (zz * 2 + yy) * 2 + kk

    def user_peer(zz, yy, kk):
        return {"user": user_at(zz, yy, kk)}

    def item_peer(xx, yy):
        return {"item": xx * 2 + yy}

    sib, yn = user_peer(z, yl, ko), user_peer(z, yo, k)
    zup, zdn, zfar = user_peer(zp, yl, k), user_peer(zm, yl, k), user_peer(z2, yl, k)
    zup_o, zdn_o = user_peer(zp, yo, k), user_peer(zm, yo, k)
    hn = item_peer(x, ho)
    xup, xdn, xfar = item_peer(xp, yh), item_peer(xm, yh), item_peer(x2, yh)
    peers = (sib, yn, zup, zdn, zfar, zup_o, zdn_o, hn, xup, xdn, xfar)

    barrier = pltpu.get_barrier_semaphore()
    for peer in peers:
        pl.semaphore_signal(barrier, inc=1, device_id=peer, device_id_type=MESH)

    pairs = (
        (item_table_h, item_table), (user_table_h, user_table), (edge_users_h, edge_users),
        (edge_items_h, edge_items), (negatives_h, negatives),
        (user_state_h, user_state), (item_state_h, item_state),
    )
    loads = [
        pltpu.make_async_copy(src, dst, load_sem.at[n]) for n, (src, dst) in enumerate(pairs)
    ]
    for load in loads:
        load.start()

    step = pl.when(u >= 0)

    copies = []

    def send(src, dst, peer):
        n = len(copies)
        copy = pltpu.make_async_remote_copy(
            src_ref=src, dst_ref=dst, send_sem=send_sem.at[n], recv_sem=recv_sem.at[n],
            device_id=peer, device_id_type=MESH,
        )
        copies.append(copy)
        copy.start()
        return copy

    def share(ref, peer):
        return send(ref, ref, peer)

    loads[0].wait()
    items[u] = item_table[...].astype(BF)
    loads[1].wait()
    users[t] = user_table[...].astype(BF)
    pl.semaphore_wait(barrier, len(peers))

    own_i, own_u = items.at[u], users.at[t]
    m_sib = share(own_i, sib)
    m_yn = share(own_i, yn)
    m_far = share(own_i, zfar)
    m_up = share(own_i, zup)
    m_dn = share(own_i, zdn)
    m_hn = share(own_u, hn)
    m_xup = share(own_u, xup)
    m_xdn = share(own_u, xdn)
    m_xfar = share(own_u, xfar)

    for load in loads[2:]:
        load.wait()
    @step
    def _():
        turn[...] = jnp.zeros_like(turn)
        item_tiles, neg_tiles = EDGES // 128, NEG // 128
        for b in range(item_tiles):
            part = slice(128 * b, 128 * (b + 1))
            turn[b:b + 1, :] = edge_items[0, :, part]
            turn[item_tiles + neg_tiles + b:item_tiles + neg_tiles + b + 1, :] = edge_users[0, :, part]
        for b in range(neg_tiles):
            turn[item_tiles + b:item_tiles + b + 1, :] = negatives[:, 128 * b:128 * (b + 1)]
        turned = turn[...].T
        for b in range(item_tiles + neg_tiles):
            item_col[128 * b:128 * (b + 1), :] = jnp.broadcast_to(turned[:, b:b + 1], (128, 128))
        for b in range(item_tiles):
            c = item_tiles + neg_tiles + b
            user_col[128 * b:128 * (b + 1), :] = jnp.broadcast_to(turned[:, c:c + 1], (128, 128))
        item_row[:, :EDGES] = edge_items[0, :, :]
        item_row[:, EDGES:] = negatives[...]

    def pick_half(zz, yy, first=False):
        @step
        def _():
            place = zz * 2 + yy
            half = items[pl.ds(place * 2, 2)].reshape(2 * IR, D)
            for b in range(PICKS // BLK):
                rows = pl.ds(b * BLK, BLK)
                one_hot = one_hot_cols(item_col[rows, :] - place * (2 * IR), 2 * IR)
                got = jnp.dot(one_hot, half, preferred_element_type=F32)
                picked[rows, :] = got if first else picked[rows, :] + got

    def item_shard(zz, yy):
        return items.at[user_at(zz, yy, k)]

    m_sib.wait_recv()
    pick_half(z, yl, True)

    m_yn.wait_recv()
    m_yup = share(item_shard(z, yo), zup)
    m_ydn = share(item_shard(z, yo), zdn)
    f_yn = share(item_shard(z, yo), sib)
    m_hn.wait_recv()
    near = users.at[x * 2 + ho]
    m_hup = share(near, xup)
    m_hdn = share(near, xdn)
    m_hfar = share(near, xfar)
    m_far.wait_recv()
    m_fary = share(item_shard(z2, yl), yn)
    f_far = share(item_shard(z2, yl), sib)
    m_up.wait_recv()
    f_dn = share(item_shard(zm, yl), sib)
    m_dn.wait_recv()
    f_up = share(item_shard(zp, yl), sib)

    f_yn.wait_recv()
    pick_half(z, yo)
    f_far.wait_recv()
    pick_half(z2, yl)
    f_dn.wait_recv()
    pick_half(zm, yl)
    m_yup.wait_recv()
    f_ydn = share(item_shard(zm, yo), sib)
    m_ydn.wait_recv()
    f_yup = share(item_shard(zp, yo), sib)
    f_up.wait_recv()
    pick_half(zp, yl)

    for copy in (m_xup, m_xdn, m_xfar, m_hup, m_hdn, m_hfar):
        copy.wait_recv()
    @step
    def _():
        for b in range(EDGES // BLK):
            rows = pl.ds(b * BLK, BLK)
            one_hot = one_hot_cols(user_col[rows, :], 8 * UR)
            got = jnp.dot(one_hot, users[...].reshape(8 * UR, D), preferred_element_type=F32)
            picked_users[rows, :] = got.astype(BF)

    m_fary.wait_recv()
    f_fary = share(item_shard(z2, yo), sib)
    f_ydn.wait_recv()
    pick_half(zm, yo)
    f_yup.wait_recv()
    pick_half(zp, yo)
    f_fary.wait_recv()
    pick_half(z2, yo)

    @step
    def _():
        picked_negs[...] = picked[EDGES:, :].astype(BF)
        for b in range(EDGES // BLK):
            rows = pl.ds(b * BLK, BLK)
            mine = picked_users[rows, :]
            wide = mine.astype(F32)
            item = picked[rows, :]
            scores = lax.dot_general(
                mine, picked_negs[...], (((1,), (1,)), ((), ())), preferred_element_type=F32
            )
            weights[rows, :] = (jax.nn.sigmoid(scores) * (1.0 / NEG)).astype(BF)
            positive = jnp.sum(wide * item, axis=1, keepdims=True)
            pull = jax.nn.sigmoid(-positive)
            picked[rows, :] = -pull * item
            item_grad[rows, :] = (-pull * wide).astype(BF)
        item_grad[EDGES:, :] = lax.dot_general(
            weights[...], picked_users[...], (((0,), (0,)), ((), ())), preferred_element_type=F32
        ).astype(BF)

    def spread_items(zz, yy, kk):
        one_hot = one_hot_rows(item_row[...], user_at(zz, yy, kk) * IR, IR)
        return jnp.dot(one_hot, item_grad[...], preferred_element_type=F32)

    def for_sib(n, places):
        @step
        def _():
            for m, (zz, yy) in enumerate(places):
                sib_s[n, m] = spread_items(zz, yy, ko).astype(BF)

        several = pl.ds(0, len(places))
        return send(sib_s.at[n, several], sib_r.at[n, several], sib)

    def for_core(n, places):
        @step
        def _():
            for m, (zz, yy) in enumerate(places):
                keep[n, m] = spread_items(zz, yy, k)

    def to_owners(n, copy, peers, joined=False):
        copy.wait_recv()

        @step
        def _():
            for m in range(len(peers)):
                total = keep[n, m] + sib_r[n, m].astype(F32)
                if joined:
                    total = total + zr[0, m].astype(F32)
                zs[n, m] = total.astype(BF)

        return [send(zs.at[n, m], zr.at[n, m], peer) for m, peer in enumerate(peers)]

    far_two, own_one = ((z2, yl), (z2, yo)), ((z, yo),)
    c0 = for_sib(0, far_two)
    for_core(0, far_two)
    c4 = for_sib(4, own_one)
    o0 = to_owners(0, c0, (zup, zdn))
    for_core(4, own_one)
    o4 = to_owners(4, c4, (yn,))

    @step
    def _():
        for b in range(EDGES // BLK):
            rows = pl.ds(b * BLK, BLK)
            user_grad[rows, :] = (
                picked[rows, :]
                + jnp.dot(weights[rows, :], picked_negs[...], preferred_element_type=F32)
            ).astype(BF)

    def spread_users(xx):
        one_hot = one_hot_rows(edge_users[0, :, :], xx * (2 * UR), 2 * UR)
        got = jnp.dot(one_hot, user_grad[...], preferred_element_type=F32)
        return got.reshape(2, UR, D)

    x_copies, x_same = [], []
    for n, (xx, peer) in enumerate(((x2, xfar), (xp, xup), (xm, xdn))):
        @step
        def _():
            uxs[n] = spread_users(xx).astype(BF)

        x_copies.append(send(uxs.at[n, ho], uxr.at[n, ho], peer))
        x_same.append((n, peer))

    @step
    def _():
        user_keep[...] = spread_users(x)


    x_same = [send(uxs.at[n, yh], uxr.at[n, yh], peer) for n, peer in x_same]
    alone_two = ((zp, yo), (zm, yl))
    c1 = for_sib(1, alone_two)
    for_core(1, alone_two)
    o1 = to_owners(1, c1, (zup_o, zdn))
    joined_two = ((zp, yl), (zm, yo))
    c2 = for_sib(2, joined_two)
    for_core(2, joined_two)
    o0[0].wait_recv()
    o0[1].wait_recv()
    o2 = to_owners(2, c2, (zup, zdn_o), True)
    c3 = for_sib(3, ((z, yl),))

    for copy in x_copies:
        copy.wait_recv()
    @step
    def _():
        uys[...] = (
            user_keep[ho] + uxr[0, ho].astype(F32) + uxr[1, ho].astype(F32) + uxr[2, ho].astype(F32)
        ).astype(BF)

    m_uy = send(uys, uyr, hn)
    for_core(3, ((z, yl),))
    for copy in x_same:
        copy.wait_recv()

    m_uy.wait_recv()
    user_total = (
        user_keep[yh] + uxr[0, yh].astype(F32) + uxr[1, yh].astype(F32) + uxr[2, yh].astype(F32)
        + uyr[...].astype(F32)
    )
    adagrad(user_table, user_state, user_total, new_user_table, new_user_state)

    c3.wait_recv()
    item_total = keep[3, 0] + sib_r[3, 0].astype(F32)
    arrivals = ((4, 0, o4[0]), (1, 0, o1[0]), (1, 1, o1[1]), (2, 0, o2[0]), (2, 1, o2[1]))
    for n, m, copy in arrivals:
        copy.wait_recv()
        item_total = item_total + zr[n, m].astype(F32)
    adagrad(item_table, item_state, item_total, new_item_table, new_item_state)
    for copy in copies:
        copy.wait_send()


MESSAGES = 48


def store(*refs):
    sources, targets, sem = refs[:4], refs[4:8], refs[8]
    moves = [
        pltpu.make_async_copy(a, b, sem.at[n]) for n, (a, b) in enumerate(zip(sources, targets))
    ]
    for move in moves:
        move.start()
    for move in moves:
        move.wait()


def per_device(user_table, user_state, item_table, item_state, edge_users, edge_items, negatives):
    vmem = pl.BlockSpec(memory_space=pltpu.VMEM)
    hbm = pl.BlockSpec(memory_space=pltpu.HBM)
    local = [
        ((UR, D), F32), ((1, UR), F32), ((IR, D), F32), ((1, IR), F32),
        ((1, 1, EDGES), jnp.int32), ((1, 1, EDGES), jnp.int32), ((1, NEG), jnp.int32),
    ]
    scratch = [
        ((16, IR, D), BF),
        ((8, UR, D), BF),
        ((128, 128), jnp.int32),
        ((EDGES, 128), jnp.int32),
        ((PICKS, 128), jnp.int32),
        ((1, PICKS), jnp.int32),
        ((PICKS, D), F32),
        ((EDGES, D), BF),
        ((NEG, D), BF),
        ((EDGES, NEG), BF),
        ((EDGES, D), BF),
        ((PICKS, D), BF),
        ((2, UR, D), F32),
        ((3, 2, UR, D), BF),
        ((3, 2, UR, D), BF),
        ((UR, D), BF),
        ((UR, D), BF),
        ((5, 2, IR, D), F32),
        ((5, 2, IR, D), BF),
        ((5, 2, IR, D), BF),
        ((5, 2, IR, D), BF),
        ((5, 2, IR, D), BF),
    ]
    shapes = [jax.ShapeDtypeStruct(shape, kind) for shape, kind in local[:4]]
    out = pl.pallas_call(
        kernel,
        out_shape=[pltpu.VMEM(shape, kind) for shape, kind in local[:4]],
        in_specs=[hbm] * 7,
        out_specs=[vmem] * 4,
        scratch_shapes=[pltpu.VMEM(shape, kind) for shape, kind in local]
        + [pltpu.SemaphoreType.DMA((7,))]
        + [pltpu.VMEM(shape, kind) for shape, kind in scratch]
        + [pltpu.SemaphoreType.DMA((MESSAGES,)), pltpu.SemaphoreType.DMA((MESSAGES,))],
        compiler_params=pltpu.CompilerParams(
            collective_id=0, has_side_effects=True, vmem_limit_bytes=48 * 1024 * 1024
        ),
        name="step",
    )(
        *(
            pltpu.with_memory_space_constraint(a, pltpu.HBM)
            for a in (
                user_table, user_state.reshape(1, UR), item_table, item_state.reshape(1, IR),
                edge_users, edge_items, negatives,
            )
        )
    )
    out = pl.pallas_call(
        store,
        out_shape=shapes,
        in_specs=[vmem] * 4,
        out_specs=[hbm] * 4,
        scratch_shapes=[pltpu.SemaphoreType.DMA((4,))],
        compiler_params=pltpu.CompilerParams(vmem_limit_bytes=16 * 1024 * 1024),
        name="store",
    )(*(pltpu.with_memory_space_constraint(a, pltpu.VMEM) for a in out))
    return (out[0], out[1].reshape(UR), out[2], out[3].reshape(IR))


def solution(mesh):
    in_specs = (
        P(("user", "item"), None),
        P(("user", "item")),
        P(("item", "user"), None),
        P(("item", "user")),
        P("user", "item", None),
        P("user", "item", None),
        P("item", None),
    )
    out_specs = (
        P(("user", "item"), None),
        P(("user", "item")),
        P(("item", "user"), None),
        P(("item", "user")),
    )
    return jax.shard_map(
        per_device, mesh=mesh, in_specs=in_specs, out_specs=out_specs, check_vma=False
    )
```
